32 devices in a mesh: dp: 2 (over x), section: 2 (over core), grid: 8 (over z, y).
Axes of the slice: x: 2, y: 2, z: 4, core: 2. Of those that a mesh axis runs over, the one named last changes fastest.
Arguments:
- section_edges: bfloat16 [2, 2, 16, 512, 768], P('section', None, ('dp', 'grid')), may hold values from -6 to 6
- lengths: int32 [2, 16], P(None, ('dp', 'grid')), may hold values from 128 to 512, as said below
- joint_weight: bfloat16 [2, 768, 2304], P('section', 'grid'), may hold values from -0.21875 to 0.21875
- query_bias: float32 [2, 768], P('section'), may hold values from -3 to 3
- value_bias: float32 [2, 768], P('section'), may hold values from -3 to 3
- output_weight: bfloat16 [2, 768, 768], P('section', 'grid'), may hold values from -1.75 to 1.75
- output_bias: float32 [2, 768], P('section'), may hold values from -2 to 2
- first_gain: float32 [2, 768], P('section'), may hold values from 0.25 to 1.75
- first_shift: float32 [2, 768], P('section'), may hold values from -2 to 2
- expand_weight: bfloat16 [2, 768, 3072], P('section', 'grid'), may hold values from -0.21875 to 0.21875
- expand_bias: float32 [2, 3072], P('section'), may hold values from -3 to 3
- reduce_weight: bfloat16 [2, 3072, 768], P('section', 'grid'), may hold values from -0.109375 to 0.109375
- reduce_bias: float32 [2, 768], P('section'), may hold values from -2 to 2
- second_gain: float32 [2, 768], P('section'), may hold values from 0.25 to 1.75
- second_shift: float32 [2, 768], P('section'), may hold values from -2 to 2
Outputs:
- boundary: float32 [2, 2, 16, 512, 768], P('section', None, ('dp', 'grid'))
- joint_weight_grad: float32 [2, 768, 2304], P('section', 'grid')
- query_bias_grad: float32 [2, 768], P('section')
- value_bias_grad: float32 [2, 768], P('section')
- output_weight_grad: float32 [2, 768, 768], P('section', 'grid')
- output_bias_grad: float32 [2, 768], P('section')
- first_gain_grad: float32 [2, 768], P('section')
- first_shift_grad: float32 [2, 768], P('section')
- expand_weight_grad: float32 [2, 768, 3072], P('section', 'grid')
- expand_bias_grad: float32 [2, 3072], P('section')
- reduce_weight_grad: float32 [2, 3072, 768], P('section', 'grid')
- reduce_bias_grad: float32 [2, 768], P('section')
- second_gain_grad: float32 [2, 768], P('section')
- second_shift_grad: float32 [2, 768], P('section')
The draws below stay inside these ranges and needn't reach their ends.
Inputs may be any that keep to these rules, and one draw needn't show every extreme that they name: `lengths`: in each micro-batch one sequence has exactly 512 valid tokens and another exactly a quarter of 512.
All inputs are finite; a program needn't handle non-finite values.
Results may differ from the reference program's by a relative error of at most 0.017.
Values may be sent and summed in bfloat16 or wider, within the bound.
A program may use at most 256 MiB of HBM per device.

```python
import jax
import jax.numpy as jnp
from jax import lax

D = 768
HEADS = 12
FF = 3072
L = 512
MICRO = 2
SEQS = 16


def draw_lengths(key, part):
    key = jax.random.fold_in(key, 11)
    base = jax.random.randint(key, (MICRO, SEQS), L // 4, L + 1)
    chosen = jax.random.randint(jax.random.fold_in(key, 1), (MICRO, 1), 0, SEQS)
    places = lax.broadcasted_iota(jnp.int32, (MICRO, SEQS), 1)
    base = jnp.where(places == chosen, L, base)
    neighbour = (chosen + 1) % SEQS
    return jnp.where(places == neighbour, L // 4, base).astype(jnp.int32)


def steps_of(stream_key, extent, cuts, low, high):
    loudness, own = 1.0, jax.random.fold_in(stream_key, 6)
    for position, parts in cuts:
        steps = jnp.exp(jax.random.uniform(jax.random.fold_in(own, position), (parts,), jnp.float32, low / len(cuts), high / len(cuts)))
        loudness = loudness * jnp.repeat(steps, extent[position] // parts).reshape([-1 if axis == position else 1 for axis in range(len(extent))])
    return loudness


def scatter_about(own_key, extent, deviation, limit, cuts=(), dtype=jnp.bfloat16):
    level = steps_of(own_key, extent, cuts, -0.22, 0.18) if cuts else 1.0
    drawn = jax.random.normal(own_key, extent, jnp.float32) * deviation * level
    return jnp.minimum(jnp.maximum(drawn, -limit), limit).astype(dtype)


def setup_inputs(seed: int = 0) -> dict:
    key_list = jax.random.split(jax.random.key(seed), 16)
    return {
        "section_edges": scatter_about(key_list[0], (2, MICRO, SEQS, L, D), 1.0, 6.0, ((0, 2), (2, 16))),
        "lengths": draw_lengths(jax.random.fold_in(key_list[15], 71), 0),
        "joint_weight": scatter_about(key_list[2], (2, D, 3 * D), D ** -0.5, 0.21875, ((0, 2), (1, 8))),
        "query_bias": scatter_about(key_list[3], (2, D), 0.5, 3.0, ((0, 2),), jnp.float32),
        "value_bias": scatter_about(key_list[4], (2, D), 0.5, 3.0, ((0, 2),), jnp.float32),
        "output_weight": scatter_about(key_list[5], (2, D, D), (max(D // 64, 1)) ** -0.5, 1.75, ((0, 2), (1, 8))),
        "output_bias": scatter_about(key_list[6], (2, D), 0.3, 2.0, ((0, 2),), jnp.float32),
        "first_gain": jnp.clip(1.0 + 0.15 * jax.random.normal(key_list[7], (2, D), jnp.float32), 0.25, 1.75),
        "first_shift": scatter_about(key_list[8], (2, D), 0.3, 2.0, ((0, 2),), jnp.float32),
        "expand_weight": scatter_about(key_list[9], (2, D, FF), D ** -0.5, 0.21875, ((0, 2), (1, 8))),
        "expand_bias": scatter_about(key_list[10], (2, FF), 0.5, 3.0, ((0, 2),), jnp.float32),
        "reduce_weight": scatter_about(key_list[11], (2, FF, D), FF ** -0.5, 0.109375, ((0, 2), (1, 8))),
        "reduce_bias": scatter_about(key_list[12], (2, D), 0.3, 2.0, ((0, 2),), jnp.float32),
        "second_gain": jnp.clip(1.0 + 0.15 * jax.random.normal(key_list[13], (2, D), jnp.float32), 0.25, 1.75),
        "second_shift": scatter_about(key_list[14], (2, D), 0.3, 2.0, ((0, 2),), jnp.float32),
    }


EPSILON = 1e-06
MASKED = -1000000000.0
HIGHEST_PRECISION = lax.Precision.HIGHEST

@jax.custom_vjp
def low(v):
    return lax.optimization_barrier(v.astype(jnp.bfloat16)).astype(jnp.float32)

@jax.custom_vjp
def low_back(v):
    return v

def low_keep(v):
    return (low(v), None)

def low_pass(kept, grad):
    return (grad,)

def back_keep(v):
    return (v, None)

def back_low(kept, grad):
    return (low(grad),)
low.defvjp(low_keep, low_pass)
low_back.defvjp(back_keep, back_low)

def norm(residual, gain_vector, shift_vector):
    center = residual - lax.optimization_barrier(jnp.mean(residual, axis=-1, keepdims=True))
    inverse = lax.rsqrt(lax.optimization_barrier(jnp.mean(center * center, axis=-1, keepdims=True)) + EPSILON)
    return center * inverse * gain_vector + shift_vector

def attend(pieces):
    query_heads, key_heads, value_heads, length = pieces
    score_scale = query_heads.shape[-1] ** (-0.5)
    raw_scores = jnp.einsum('qhe,khe->hqk', query_heads, key_heads, precision=HIGHEST_PRECISION) * score_scale
    places = lax.broadcasted_iota(jnp.int32, raw_scores.shape, 2)
    scores = low_back(jnp.where(places < length, raw_scores, MASKED))
    probabilities = low(jax.nn.softmax(scores, axis=-1))
    return jnp.einsum('hqk,khe->qhe', probabilities, value_heads, precision=HIGHEST_PRECISION)

def layer(hidden, seq_lengths, params):
    joint_matrix, query_bias, value_bias, output_matrix, output_bias, first_gain, first_shift, expand_matrix, expand_bias, reduce_matrix, reduce_bias, second_gain, second_shift = params
    seq_count, seq_span, model_width = hidden.shape
    flat_rows = hidden.reshape(seq_count * seq_span, model_width)
    bias_row = jnp.concatenate([query_bias, jnp.zeros_like(query_bias), value_bias])
    projected = low_back(low(jnp.dot(flat_rows, joint_matrix, precision=HIGHEST_PRECISION) + bias_row))
    heads_split = projected.reshape(seq_count, seq_span, 3, HEADS, model_width // HEADS)
    attended = lax.map(jax.checkpoint(attend), (heads_split[:, :, 0], heads_split[:, :, 1], heads_split[:, :, 2], seq_lengths))
    attended = low_back(low(attended.reshape(seq_count * seq_span, model_width)))
    branch = low_back(jnp.dot(attended, output_matrix, precision=HIGHEST_PRECISION) + output_bias)
    normal_first = norm(flat_rows + branch, first_gain, first_shift)
    preact = low_back(jnp.dot(low(normal_first), expand_matrix, precision=HIGHEST_PRECISION) + expand_bias)
    activation = low(jax.nn.gelu(preact, approximate=False))
    branch_second = low_back(jnp.dot(activation, reduce_matrix, precision=HIGHEST_PRECISION) + reduce_bias)
    output = norm(normal_first + branch_second, second_gain, second_shift)
    return output.reshape(seq_count, seq_span, model_width)

def reference(section_edges, lengths, joint_weight, query_bias, value_bias, output_weight, output_bias, first_gain, first_shift, expand_weight, expand_bias, reduce_weight, reduce_bias, second_gain, second_shift):
    inputs = section_edges[0].astype(jnp.float32)
    cotangent = section_edges[1].astype(jnp.float32)
    micro_count, seq_count, seq_span, model_width = inputs.shape
    flat_lengths = lengths.reshape(-1).astype(jnp.int32)
    params = tuple((w.astype(jnp.float32) for w in (joint_weight, query_bias, value_bias, output_weight, output_bias, first_gain, first_shift, expand_weight, expand_bias, reduce_weight, reduce_bias, second_gain, second_shift)))

    def forward(layer_input, weights):
        hidden = layer_input.reshape(micro_count * seq_count, seq_span, model_width)
        first_out = layer(hidden, flat_lengths, tuple((w[0] for w in weights)))
        passed = low_back(low(first_out))
        return layer(passed, flat_lengths, tuple((w[1] for w in weights))).reshape(layer_input.shape)
    output, backward_fn = jax.vjp(forward, inputs, params)
    grad_inputs, grads = backward_fn(cotangent)
    factor = float(micro_count * seq_count * seq_span) ** (-0.5)
    boundary = jnp.stack([grad_inputs, output])
    return (boundary, grads[0] * factor, grads[1] * factor, grads[2] * factor, grads[3] * factor, grads[4] * factor, grads[5] * factor, grads[6] * factor, grads[7] * factor, grads[8] * factor, grads[9] * factor, grads[10] * factor, grads[11] * factor, grads[12] * factor)
```

```python
import math

import jax
import jax.numpy as jnp
from jax import lax
from jax.experimental import pallas as pl
from jax.experimental.pallas import tpu as pltpu
from jax.sharding import PartitionSpec as P

HEADS = 12


EPSILON = 1e-06
MASKED = -1000000000.0
LANES = 128
LOWER = jnp.bfloat16
WIDE = jnp.float32


def norm_forward(residual, gain_vector, shift_vector):
    center = residual - jnp.mean(residual, axis=-1, keepdims=True)
    inverse = lax.rsqrt(jnp.mean(center * center, axis=-1, keepdims=True) + EPSILON)
    normed = center * inverse
    return (normed * gain_vector + shift_vector, normed, inverse)


def norm_backward(gradient, normed, inverse, gain_vector):
    scaled = gradient * gain_vector
    return inverse * (
        scaled
        - jnp.mean(scaled, axis=-1, keepdims=True)
        - normed * jnp.mean(scaled * normed, axis=-1, keepdims=True)
    )


def times_transposed(left_rows, right_rows):
    return lax.dot_general(
        left_rows, right_rows, (((1,), (1,)), ((), ())), preferred_element_type=WIDE
    )


def over_contract(left, right, left_dim, right_dim):
    return lax.dot_general(
        left, right, (((left_dim,), (right_dim,)), ((), ())), preferred_element_type=WIDE
    )


def head_softmax(query, key, length, score_scale):
    scores = over_contract(query, key, 1, 1) * score_scale
    places = lax.broadcasted_iota(jnp.int32, scores.shape, 1)
    scores = jnp.where(places < length, scores, MASKED)
    weights = jnp.exp(scores - jnp.max(scores, axis=-1, keepdims=True))
    return weights * (1.0 / jnp.sum(weights, axis=-1, keepdims=True))


def attend_kernel(head_width, lengths_ref, query_ref, key_ref, value_ref, out_ref):
    length = lengths_ref[pl.program_id(0)]
    query, key, value = query_ref[...], key_ref[...], value_ref[...]
    lane = lax.broadcasted_iota(jnp.int32, query.shape, 1)
    total = jnp.zeros(query.shape, WIDE)
    for part in range(LANES // head_width):
        own = lane // head_width == part
        probs = head_softmax(
            jnp.where(own, query, jnp.zeros_like(query)), key, length, head_width ** (-0.5)
        )
        own_value = jnp.where(own, value, jnp.zeros_like(value))
        total = total + over_contract(probs.astype(LOWER), own_value, 1, 0)
    out_ref[...] = total.astype(LOWER)


def attend_backward_kernel(
    head_width, lengths_ref, query_ref, key_ref, value_ref, grad_ref, out_ref
):
    length = lengths_ref[pl.program_id(0)]
    pair = pl.program_id(1)
    model_width = out_ref.shape[1] // 3
    query, key, value, grad = query_ref[...], key_ref[...], value_ref[...], grad_ref[...]
    lane = lax.broadcasted_iota(jnp.int32, query.shape, 1)
    score_scale = head_width ** (-0.5)
    grad_query = jnp.zeros(query.shape, WIDE)
    grad_key = jnp.zeros(query.shape, WIDE)
    grad_value = jnp.zeros(query.shape, WIDE)
    none = jnp.zeros_like(query)
    for part in range(LANES // head_width):
        own = lane // head_width == part
        own_query = jnp.where(own, query, none)
        own_key = jnp.where(own, key, none)
        own_grad = jnp.where(own, grad, none)
        probs = head_softmax(own_query, key, length, score_scale)
        grad_probs = over_contract(own_grad, value, 1, 1)
        row_term = jnp.sum(grad_probs * probs, axis=-1, keepdims=True)
        grad_scores = (probs * (grad_probs - row_term)).astype(LOWER)
        grad_value = grad_value + over_contract(probs.astype(LOWER), own_grad, 0, 0)
        grad_query = grad_query + over_contract(grad_scores, own_key, 1, 0)
        grad_key = grad_key + over_contract(grad_scores, own_query, 0, 0)
    for place, result in enumerate(
        (grad_query * score_scale, grad_key * score_scale, grad_value)
    ):
        start = pl.multiple_of(place * model_width + pair * LANES, LANES)
        out_ref[:, pl.ds(start, LANES)] = result.astype(LOWER)


def head_blocks(span, first):
    return pl.BlockSpec((span, LANES), lambda s, i: (s, first + i))


def attention(projected, seq_lengths):
    row_count, width = projected.shape
    model_width = width // 3
    seq_count = seq_lengths.shape[0]
    span = row_count // seq_count
    pairs = model_width // LANES
    head_width = model_width // HEADS

    def kernel(*refs):
        attend_kernel(head_width, *refs)

    return pl.pallas_call(
        kernel,
        grid=(seq_count, pairs),
        in_specs=[
            pl.BlockSpec(memory_space=pltpu.SMEM),
            head_blocks(span, 0),
            head_blocks(span, pairs),
            head_blocks(span, 2 * pairs),
        ],
        out_specs=head_blocks(span, 0),
        out_shape=jax.ShapeDtypeStruct((row_count, model_width), LOWER),
        compiler_params=pltpu.CompilerParams(vmem_limit_bytes=32 * 1024 * 1024),
        cost_estimate=pl.CostEstimate(
            flops=8 * row_count * span * model_width,
            bytes_accessed=8 * row_count * model_width,
            transcendentals=row_count * span * HEADS,
        ),
    )(seq_lengths, projected, projected, projected)


def attention_backward(projected, grad_attended, seq_lengths):
    row_count, width = projected.shape
    model_width = width // 3
    seq_count = seq_lengths.shape[0]
    span = row_count // seq_count
    pairs = model_width // LANES
    head_width = model_width // HEADS

    def kernel(*refs):
        attend_backward_kernel(head_width, *refs)

    return pl.pallas_call(
        kernel,
        grid=(seq_count, pairs),
        in_specs=[
            pl.BlockSpec(memory_space=pltpu.SMEM),
            head_blocks(span, 0),
            head_blocks(span, pairs),
            head_blocks(span, 2 * pairs),
            head_blocks(span, 0),
        ],
        out_specs=pl.BlockSpec((span, width), lambda s, i: (s, 0)),
        out_shape=jax.ShapeDtypeStruct((row_count, width), LOWER),
        compiler_params=pltpu.CompilerParams(vmem_limit_bytes=48 * 1024 * 1024),
        cost_estimate=pl.CostEstimate(
            flops=20 * row_count * span * model_width,
            bytes_accessed=14 * row_count * model_width,
            transcendentals=row_count * span * HEADS,
        ),
    )(seq_lengths, projected, projected, projected, grad_attended)


def layer_forward(inputs, seq_lengths, matrices, vectors):
    joint_matrix, output_matrix, expand_matrix, reduce_matrix = matrices
    (
        query_bias,
        value_bias,
        output_bias,
        first_gain,
        first_shift,
        reduce_bias,
        second_gain,
        second_shift,
        expand_bias,
    ) = vectors
    bias_row = jnp.concatenate([query_bias, jnp.zeros_like(query_bias), value_bias])
    projected = (jnp.dot(inputs, joint_matrix, preferred_element_type=WIDE) + bias_row).astype(
        LOWER
    )
    attended = attention(projected, seq_lengths)
    residual_one = inputs.astype(WIDE) + (
        jnp.dot(attended, output_matrix, preferred_element_type=WIDE) + output_bias
    )
    normal_first, normed_first, inverse_first = norm_forward(residual_one, first_gain, first_shift)
    normal_low = normal_first.astype(LOWER)
    preact = jnp.dot(normal_low, expand_matrix, preferred_element_type=WIDE) + expand_bias
    below = 0.5 * (1.0 + lax.erf(preact * math.sqrt(0.5)))
    activation = (preact * below).astype(LOWER)
    slope = below + preact * (jnp.exp(-0.5 * preact * preact) * (1.0 / math.sqrt(2.0 * math.pi)))
    residual_two = normal_first + (
        jnp.dot(activation, reduce_matrix, preferred_element_type=WIDE) + reduce_bias
    )
    output, normed_second, inverse_second = norm_forward(residual_two, second_gain, second_shift)
    stored = (
        inputs,
        projected,
        attended,
        normed_first,
        inverse_first,
        normal_low,
        slope,
        activation,
        normed_second,
        inverse_second,
    )
    return (output, stored)


def layer_backward(gradient, stored, seq_lengths, matrices, vectors):
    (
        inputs,
        projected,
        attended,
        normed_first,
        inverse_first,
        normal_low,
        slope,
        activation,
        normed_second,
        inverse_second,
    ) = stored
    joint_matrix, output_matrix, expand_matrix, reduce_matrix = matrices
    first_gain = vectors[3]
    second_gain = vectors[6]
    model_width = inputs.shape[1]
    grad_second = norm_backward(gradient, normed_second, inverse_second, second_gain)
    second_gain_term = jnp.sum(gradient * normed_second, axis=0)
    second_shift_term = jnp.sum(gradient, axis=0)
    grad_branch_two = grad_second.astype(LOWER)
    reduce_bias_term = jnp.sum(grad_branch_two.astype(WIDE), axis=0)
    grad_preact = (times_transposed(grad_branch_two, reduce_matrix) * slope).astype(LOWER)
    expand_bias_term = jnp.sum(grad_preact.astype(WIDE), axis=0)
    grad_normal = grad_second + times_transposed(grad_preact, expand_matrix)
    grad_first = norm_backward(grad_normal, normed_first, inverse_first, first_gain)
    first_gain_term = jnp.sum(grad_normal * normed_first, axis=0)
    first_shift_term = jnp.sum(grad_normal, axis=0)
    grad_branch_one = grad_first.astype(LOWER)
    output_bias_term = jnp.sum(grad_branch_one.astype(WIDE), axis=0)
    grad_attended = times_transposed(grad_branch_one, output_matrix).astype(LOWER)
    grad_projected = attention_backward(projected, grad_attended, seq_lengths)
    column_sums = jnp.sum(grad_projected.astype(WIDE), axis=0)
    grad_inputs = grad_first + times_transposed(grad_projected, joint_matrix)
    products = tuple(
        over_contract(left, right, 0, 0).astype(LOWER)
        for left, right in (
            (inputs, grad_projected),
            (attended, grad_branch_one),
            (normal_low, grad_preact),
            (activation, grad_branch_two),
        )
    )
    vector_terms = jnp.concatenate(
        [
            column_sums[:model_width],
            column_sums[2 * model_width :],
            output_bias_term,
            first_gain_term,
            first_shift_term,
            reduce_bias_term,
            second_gain_term,
            second_shift_term,
            expand_bias_term,
        ]
    )
    return (grad_inputs, products, vector_terms)


def swap(array, axis, distance=1):
    length = lax.axis_size(axis)
    return lax.ppermute(array, axis, [(i, i ^ distance) for i in range(length)])


def onward(array):
    length = lax.axis_size("grid")
    return lax.ppermute(array, "grid", [(i, (i + 2) % length) for i in range(length)])


def put(buffer, piece, *places):
    starts = tuple(places) + (0,) * (buffer.ndim - len(places))
    shape = (1,) * len(places) + buffer.shape[len(places) :]
    return lax.dynamic_update_slice(buffer, piece.reshape(shape), starts)


def pick(array, place, axis=0):
    return lax.dynamic_index_in_dim(array, place, axis, keepdims=False)


def gather_rows(rows, pair_first):
    size = lax.axis_size("grid")
    steps = size // 2
    here = lax.axis_index("grid")
    column, side = here // 2, here % 2
    buffer = jnp.zeros((steps, 2) + rows.shape, rows.dtype)
    moving = rows
    if pair_first:
        pair = jnp.zeros((2,) + rows.shape, rows.dtype)
        moving = put(put(pair, rows, side), swap(rows, "grid"), 1 - side)
    for step in range(steps):
        place = (column - step) % steps
        if pair_first:
            buffer = put(buffer, moving, place)
        else:
            buffer = put(buffer, moving, place, side)
            buffer = put(buffer, swap(moving, "grid"), place, 1 - side)
        if step < steps - 1:
            moving = onward(moving)
    return buffer.reshape(size * rows.shape[0], rows.shape[1])


def pair_sum(array, side, axis):
    received = swap(pick(array, 1 - side, axis).astype(LOWER), "grid")
    return pick(array, side, axis).astype(WIDE) + received.astype(WIDE)


def ring_sum(array, column):
    steps = array.shape[0]
    moving = pick(array, (column - 1) % steps).astype(WIDE)
    for step in range(steps - 1):
        received = onward(moving.astype(LOWER))
        moving = received.astype(WIDE) + pick(array, (column - 2 - step) % steps).astype(WIDE)
    return moving


def sum_rows(product, pair_last):
    size = lax.axis_size("grid")
    core = lax.axis_index("section")
    here = lax.axis_index("grid")
    column, side = here // 2, here % 2
    rows, width = product.shape
    halves = product.reshape(size // 2, 2, 2, rows // size // 2, width)
    received = swap(pick(halves, 1 - core, 2), "section")
    both = (pick(halves, core, 2).astype(WIDE) + received.astype(WIDE)).astype(LOWER)
    if pair_last:
        total = pair_sum(ring_sum(both, column), side, 0)
    else:
        total = ring_sum(pair_sum(both, side, 1).astype(LOWER), column)
    groups = lax.axis_size("dp")
    sent = total.astype(LOWER)
    for step in range(1, groups):
        received = lax.ppermute(sent, "dp", [(i, (i + step) % groups) for i in range(groups)])
        total = total + received.astype(WIDE)
    return total


def on_device(
    section_edges,
    lengths,
    joint_weight,
    query_bias,
    value_bias,
    output_weight,
    output_bias,
    first_gain,
    first_shift,
    expand_weight,
    expand_bias,
    reduce_weight,
    reduce_bias,
    second_gain,
    second_shift,
):
    core = lax.axis_index("section")
    first_core = core == 0
    edges = section_edges[0]
    micro_count, seq_count, seq_span, model_width = edges.shape
    row_count = seq_count * seq_span
    edges = edges.reshape(micro_count, row_count, model_width)
    kept_edge = pick(edges, core)
    other_edge = swap(pick(edges, 1 - core), "section")
    hidden = jnp.where(first_core, kept_edge, other_edge)
    cotangent = jnp.where(first_core, other_edge, kept_edge)
    seq_lengths = pick(lengths, core)

    def both_layers(own):
        other = swap(own, "section")
        return (jnp.where(first_core, own, other), jnp.where(first_core, other, own))

    vector_list = (
        query_bias,
        value_bias,
        output_bias,
        first_gain,
        first_shift,
        reduce_bias,
        second_gain,
        second_shift,
        expand_bias,
    )
    cuts = []
    for vector in vector_list:
        cuts.append((cuts[-1] if cuts else 0) + vector.shape[1])
    vector_layers = [
        jnp.split(layer, cuts[:-1])
        for layer in both_layers(jnp.concatenate([v[0] for v in vector_list]))
    ]
    matrix_layers = list(
        zip(
            both_layers(gather_rows(joint_weight[0], True)),
            both_layers(gather_rows(output_weight[0], False)),
            both_layers(gather_rows(expand_weight[0], False)),
            both_layers(gather_rows(reduce_weight[0], False)),
        )
    )
    stored_list = []
    for layer in range(2):
        output, stored = layer_forward(
            hidden, seq_lengths, matrix_layers[layer], vector_layers[layer]
        )
        stored_list.append(stored)
        hidden = output.astype(LOWER)
    gradient = cotangent.astype(WIDE)
    sums = [None, None]
    vector_terms = [None, None]
    for layer in (1, 0):
        gradient, products, vector_terms[layer] = layer_backward(
            gradient,
            stored_list[layer],
            seq_lengths,
            matrix_layers[layer],
            vector_layers[layer],
        )
        sums[layer] = [sum_rows(products[i], i == 0) for i in range(4)]
        if layer == 1:
            gradient = gradient.astype(LOWER).astype(WIDE)
    own_rows = jnp.where(first_core, gradient, output)
    other_rows = swap(jnp.where(first_core, output, gradient), "section")
    boundary = put(put(jnp.zeros((2,) + own_rows.shape, WIDE), own_rows, core), other_rows, 1 - core)
    boundary = boundary.reshape(1, micro_count, seq_count, seq_span, model_width)
    positions = lax.axis_size("dp") * lax.axis_size("grid")
    factor = 1.0 / math.sqrt(micro_count * row_count * positions)
    matrix_grads = []
    for index in range(4):
        first_half, second_half = sums[0][index], sums[1][index]
        kept = jnp.where(first_core, first_half, second_half)
        received = swap(jnp.where(first_core, second_half, first_half), "section")
        whole = put(put(jnp.zeros((2,) + kept.shape, WIDE), kept, core), received, 1 - core)
        matrix_grads.append((whole.reshape(-1, kept.shape[-1]) * factor)[None])
    vector_sum = jnp.where(first_core, vector_terms[0], vector_terms[1]) + swap(
        jnp.where(first_core, vector_terms[1], vector_terms[0]), "section"
    )
    for axis in ("dp", "grid"):
        distance = 1
        while distance < lax.axis_size(axis):
            vector_sum = vector_sum + swap(vector_sum, axis, distance)
            distance *= 2
    vector_grads = [part[None] for part in jnp.split(vector_sum * factor, cuts[:-1])]
    return (
        boundary,
        matrix_grads[0],
        vector_grads[0],
        vector_grads[1],
        matrix_grads[1],
        vector_grads[2],
        vector_grads[3],
        vector_grads[4],
        matrix_grads[2],
        vector_grads[8],
        matrix_grads[3],
        vector_grads[5],
        vector_grads[6],
        vector_grads[7],
    )


def solution(mesh):
    placed = (
        P("section", None, ("dp", "grid"), None, None),
        P(None, ("dp", "grid")),
        P("section", "grid", None),
        P("section", None),
        P("section", None),
        P("section", "grid", None),
        P("section", None),
        P("section", None),
        P("section", None),
        P("section", "grid", None),
        P("section", None),
        P("section", "grid", None),
        P("section", None),
        P("section", None),
        P("section", None),
    )
    return jax.shard_map(
        on_device,
        mesh=mesh,
        in_specs=placed,
        out_specs=(
            P("section", None, ("dp", "grid"), None, None),
            P("section", "grid", None),
            P("section", None),
            P("section", None),
            P("section", "grid", None),
            P("section", None),
            P("section", None),
            P("section", None),
            P("section", "grid", None),
            P("section", None),
            P("section", "grid", None),
            P("section", None),
            P("section", None),
            P("section", None),
        ),
        check_vma=False,
    )
```

```python
import math

import jax
import jax.numpy as jnp
from jax import lax
from jax.experimental import pallas as pl
from jax.experimental.pallas import tpu as pltpu
from jax.sharding import PartitionSpec as P

HEADS = 12


EPSILON = 1e-06
MASKED = -1000000000.0
LANES = 128
LOWER = jnp.bfloat16
WIDE = jnp.float32


def norm_forward(residual, gain_vector, shift_vector):
    center = residual - jnp.mean(residual, axis=-1, keepdims=True)
    inverse = lax.rsqrt(jnp.mean(center * center, axis=-1, keepdims=True) + EPSILON)
    normed = center * inverse
    return (normed * gain_vector + shift_vector, normed, inverse)


def norm_backward(gradient, normed, inverse, gain_vector):
    scaled = gradient * gain_vector
    return inverse * (
        scaled
        - jnp.mean(scaled, axis=-1, keepdims=True)
        - normed * jnp.mean(scaled * normed, axis=-1, keepdims=True)
    )


def times_transposed(left_rows, right_rows):
    return lax.dot_general(
        left_rows, right_rows, (((1,), (1,)), ((), ())), preferred_element_type=WIDE
    )


def over_contract(left, right, left_dim, right_dim):
    return lax.dot_general(
        left, right, (((left_dim,), (right_dim,)), ((), ())), preferred_element_type=WIDE
    )


def head_softmax(query, key, length, score_scale):
    scores = over_contract(query, key, 1, 1) * score_scale
    places = lax.broadcasted_iota(jnp.int32, scores.shape, 1)
    scores = jnp.where(places < length, scores, MASKED)
    weights = jnp.exp(scores - jnp.max(scores, axis=-1, keepdims=True))
    return weights * (1.0 / jnp.sum(weights, axis=-1, keepdims=True))


def attend_kernel(head_width, lengths_ref, query_ref, key_ref, value_ref, out_ref):
    length = lengths_ref[pl.program_id(0)]
    query, key, value = query_ref[...], key_ref[...], value_ref[...]
    lane = lax.broadcasted_iota(jnp.int32, query.shape, 1)
    total = jnp.zeros(query.shape, WIDE)
    for part in range(LANES // head_width):
        own = lane // head_width == part
        probs = head_softmax(
            jnp.where(own, query, jnp.zeros_like(query)), key, length, head_width ** (-0.5)
        )
        own_value = jnp.where(own, value, jnp.zeros_like(value))
        total = total + over_contract(probs.astype(LOWER), own_value, 1, 0)
    out_ref[...] = total.astype(LOWER)


def attend_backward_kernel(
    head_width, lengths_ref, query_ref, key_ref, value_ref, grad_ref, out_ref
):
    length = lengths_ref[pl.program_id(0)]
    pair = pl.program_id(1)
    model_width = out_ref.shape[1] // 3
    query, key, value, grad = query_ref[...], key_ref[...], value_ref[...], grad_ref[...]
    lane = lax.broadcasted_iota(jnp.int32, query.shape, 1)
    score_scale = head_width ** (-0.5)
    grad_query = jnp.zeros(query.shape, WIDE)
    grad_key = jnp.zeros(query.shape, WIDE)
    grad_value = jnp.zeros(query.shape, WIDE)
    none = jnp.zeros_like(query)
    for part in range(LANES // head_width):
        own = lane // head_width == part
        own_query = jnp.where(own, query, none)
        own_key = jnp.where(own, key, none)
        own_grad = jnp.where(own, grad, none)
        probs = head_softmax(own_query, key, length, score_scale)
        grad_probs = over_contract(own_grad, value, 1, 1)
        row_term = jnp.sum(grad_probs * probs, axis=-1, keepdims=True)
        grad_scores = (probs * (grad_probs - row_term)).astype(LOWER)
        grad_value = grad_value + over_contract(probs.astype(LOWER), own_grad, 0, 0)
        grad_query = grad_query + over_contract(grad_scores, own_key, 1, 0)
        grad_key = grad_key + over_contract(grad_scores, own_query, 0, 0)
    for place, result in enumerate(
        (grad_query * score_scale, grad_key * score_scale, grad_value)
    ):
        start = pl.multiple_of(place * model_width + pair * LANES, LANES)
        out_ref[:, pl.ds(start, LANES)] = result.astype(LOWER)


def head_blocks(span, first):
    return pl.BlockSpec((span, LANES), lambda s, i: (s, first + i))


def attention(projected, seq_lengths):
    row_count, width = projected.shape
    model_width = width // 3
    seq_count = seq_lengths.shape[0]
    span = row_count // seq_count
    pairs = model_width // LANES
    head_width = model_width // HEADS

    def kernel(*refs):
        attend_kernel(head_width, *refs)

    return pl.pallas_call(
        kernel,
        grid=(seq_count, pairs),
        in_specs=[
            pl.BlockSpec(memory_space=pltpu.SMEM),
            head_blocks(span, 0),
            head_blocks(span, pairs),
            head_blocks(span, 2 * pairs),
        ],
        out_specs=head_blocks(span, 0),
        out_shape=jax.ShapeDtypeStruct((row_count, model_width), LOWER),
        compiler_params=pltpu.CompilerParams(vmem_limit_bytes=32 * 1024 * 1024),
        cost_estimate=pl.CostEstimate(
            flops=8 * row_count * span * model_width,
            bytes_accessed=8 * row_count * model_width,
            transcendentals=row_count * span * HEADS,
        ),
    )(seq_lengths, projected, projected, projected)


def attention_backward(projected, grad_attended, seq_lengths):
    row_count, width = projected.shape
    model_width = width // 3
    seq_count = seq_lengths.shape[0]
    span = row_count // seq_count
    pairs = model_width // LANES
    head_width = model_width // HEADS

    def kernel(*refs):
        attend_backward_kernel(head_width, *refs)

    return pl.pallas_call(
        kernel,
        grid=(seq_count, pairs),
        in_specs=[
            pl.BlockSpec(memory_space=pltpu.SMEM),
            head_blocks(span, 0),
            head_blocks(span, pairs),
            head_blocks(span, 2 * pairs),
            head_blocks(span, 0),
        ],
        out_specs=pl.BlockSpec((span, width), lambda s, i: (s, 0)),
        out_shape=jax.ShapeDtypeStruct((row_count, width), LOWER),
        compiler_params=pltpu.CompilerParams(vmem_limit_bytes=48 * 1024 * 1024),
        cost_estimate=pl.CostEstimate(
            flops=20 * row_count * span * model_width,
            bytes_accessed=14 * row_count * model_width,
            transcendentals=row_count * span * HEADS,
        ),
    )(seq_lengths, projected, projected, projected, grad_attended)


def layer_forward(inputs, seq_lengths, matrices, vectors):
    joint_matrix, output_matrix, expand_matrix, reduce_matrix = matrices
    (
        query_bias,
        value_bias,
        output_bias,
        first_gain,
        first_shift,
        reduce_bias,
        second_gain,
        second_shift,
        expand_bias,
    ) = vectors
    bias_row = jnp.concatenate([query_bias, jnp.zeros_like(query_bias), value_bias])
    projected = (jnp.dot(inputs, joint_matrix, preferred_element_type=WIDE) + bias_row).astype(
        LOWER
    )
    attended = attention(projected, seq_lengths)
    residual_one = inputs.astype(WIDE) + (
        jnp.dot(attended, output_matrix, preferred_element_type=WIDE) + output_bias
    )
    normal_first, normed_first, inverse_first = norm_forward(residual_one, first_gain, first_shift)
    normal_low = normal_first.astype(LOWER)
    preact = jnp.dot(normal_low, expand_matrix, preferred_element_type=WIDE) + expand_bias
    below = 0.5 * (1.0 + lax.erf(preact * math.sqrt(0.5)))
    activation = (preact * below).astype(LOWER)
    slope = below + preact * (jnp.exp(-0.5 * preact * preact) * (1.0 / math.sqrt(2.0 * math.pi)))
    residual_two = normal_first + (
        jnp.dot(activation, reduce_matrix, preferred_element_type=WIDE) + reduce_bias
    )
    output, normed_second, inverse_second = norm_forward(residual_two, second_gain, second_shift)
    stored = (
        inputs,
        projected,
        attended,
        normed_first,
        inverse_first,
        normal_low,
        slope,
        activation,
        normed_second,
        inverse_second,
    )
    return (output, stored)


def layer_backward(gradient, stored, seq_lengths, matrices, vectors, sums, layer):
    (
        inputs,
        projected,
        attended,
        normed_first,
        inverse_first,
        normal_low,
        slope,
        activation,
        normed_second,
        inverse_second,
    ) = stored
    joint_matrix, output_matrix, expand_matrix, reduce_matrix = matrices
    first_gain = vectors[3]
    second_gain = vectors[6]
    model_width = inputs.shape[1]
    grad_second = norm_backward(gradient, normed_second, inverse_second, second_gain)
    second_gain_term = jnp.sum(gradient * normed_second, axis=0)
    second_shift_term = jnp.sum(gradient, axis=0)
    grad_branch_two = grad_second.astype(LOWER)

    def begin(index, left, right, pauses):
        product = over_contract(left, right, 0, 0).astype(LOWER)
        sums.start((layer, index), sum_rows(product, index == 0, pauses))

    begin(3, activation, grad_branch_two, (0, 1))
    grad_second, grad_branch_two = sums.boundary(grad_second, grad_branch_two)
    reduce_bias_term = jnp.sum(grad_branch_two.astype(WIDE), axis=0)
    grad_preact = (times_transposed(grad_branch_two, reduce_matrix) * slope).astype(LOWER)
    begin(2, normal_low, grad_preact, (1, 1))
    grad_second, grad_preact = sums.boundary(grad_second, grad_preact)
    expand_bias_term = jnp.sum(grad_preact.astype(WIDE), axis=0)
    grad_normal = grad_second + times_transposed(grad_preact, expand_matrix)
    grad_first = norm_backward(grad_normal, normed_first, inverse_first, first_gain)
    first_gain_term = jnp.sum(grad_normal * normed_first, axis=0)
    first_shift_term = jnp.sum(grad_normal, axis=0)
    grad_branch_one = grad_first.astype(LOWER)
    begin(1, attended, grad_branch_one, (1, 0))
    grad_first, grad_branch_one = sums.boundary(grad_first, grad_branch_one)
    output_bias_term = jnp.sum(grad_branch_one.astype(WIDE), axis=0)
    grad_attended = times_transposed(grad_branch_one, output_matrix).astype(LOWER)
    grad_projected = attention_backward(projected, grad_attended, seq_lengths)
    begin(0, inputs, grad_projected, (0, 0))
    grad_first, grad_projected = sums.boundary(grad_first, grad_projected)
    column_sums = jnp.sum(grad_projected.astype(WIDE), axis=0)
    grad_inputs = grad_first + times_transposed(grad_projected, joint_matrix)
    (grad_inputs,) = sums.boundary(grad_inputs)
    vector_terms = jnp.concatenate(
        [
            column_sums[:model_width],
            column_sums[2 * model_width :],
            output_bias_term,
            first_gain_term,
            first_shift_term,
            reduce_bias_term,
            second_gain_term,
            second_shift_term,
            expand_bias_term,
        ]
    )
    return (grad_inputs, vector_terms)


def swap(array, axis, distance=1):
    length = lax.axis_size(axis)
    return lax.ppermute(array, axis, [(i, i ^ distance) for i in range(length)])


def onward(array):
    length = lax.axis_size("grid")
    return lax.ppermute(array, "grid", [(i, (i + 2) % length) for i in range(length)])


def put(buffer, piece, *places):
    starts = tuple(places) + (0,) * (buffer.ndim - len(places))
    shape = (1,) * len(places) + buffer.shape[len(places) :]
    return lax.dynamic_update_slice(buffer, piece.reshape(shape), starts)


def pick(array, place, axis=0):
    return lax.dynamic_index_in_dim(array, place, axis, keepdims=False)


def after(value, *others):
    return lax.optimization_barrier((value,) + others)[0]


def gather_rows(rows, pair_first, *others):
    size = lax.axis_size("grid")
    steps = size // 2
    here = lax.axis_index("grid")
    column, side = here // 2, here % 2
    buffer = jnp.zeros((steps, 2) + rows.shape, rows.dtype)
    moving = after(rows, *others) if others else rows
    if pair_first:
        pair = jnp.zeros((2,) + rows.shape, rows.dtype)
        moving = put(put(pair, rows, side), swap(rows, "grid"), 1 - side)
    for step in range(steps):
        place = (column - step) % steps
        if pair_first:
            buffer = put(buffer, moving, place)
        else:
            buffer = put(buffer, moving, place, side)
            buffer = put(buffer, swap(moving, "grid"), place, 1 - side)
        if step < steps - 1:
            last_sent = moving
            moving = onward(moving)
    return buffer.reshape(size * rows.shape[0], rows.shape[1]), last_sent


def pair_sum(array, side, axis):
    sent = yield pick(array, 1 - side, axis).astype(LOWER)
    received = swap(sent, "grid")
    return pick(array, side, axis).astype(WIDE) + received.astype(WIDE)


def ring_sum(array, column):
    steps = array.shape[0]
    moving = pick(array, (column - 1) % steps).astype(WIDE)
    for step in range(steps - 1):
        sent = yield moving.astype(LOWER)
        received = onward(sent)
        moving = received.astype(WIDE) + pick(array, (column - 2 - step) % steps).astype(WIDE)
    return moving


def pause(count):
    for _ in range(count):
        yield None


def sum_rows(product, pair_last, pauses):
    size = lax.axis_size("grid")
    core = lax.axis_index("section")
    here = lax.axis_index("grid")
    column, side = here // 2, here % 2
    rows, width = product.shape
    halves = product.reshape(size // 2, 2, 2, rows // size // 2, width)
    sent = yield pick(halves, 1 - core, 2)
    received = swap(sent, "section")
    yield from pause(pauses[0])
    both = (pick(halves, core, 2).astype(WIDE) + received.astype(WIDE)).astype(LOWER)
    if pair_last:
        ring = yield from ring_sum(both, column)
        yield from pause(pauses[1])
        total = yield from pair_sum(ring, side, 0)
    else:
        pair = yield from pair_sum(both, side, 1)
        yield from pause(pauses[1])
        total = yield from ring_sum(pair.astype(LOWER), column)
    groups = lax.axis_size("dp")
    sent = yield total.astype(LOWER)
    for step in range(1, groups):
        received = lax.ppermute(sent, "dp", [(i, (i + step) % groups) for i in range(groups)])
        total = total + received.astype(WIDE)
    return total


class Sums:
    def __init__(self):
        self.running = {}
        self.pending = {}
        self.results = {}

    def resume(self, name, value):
        try:
            self.pending[name] = self.running[name].send(value)
        except StopIteration as stop:
            self.results[name] = stop.value
            del self.running[name]
            self.pending.pop(name, None)

    def start(self, name, generator):
        self.running[name] = generator
        self.resume(name, None)

    def boundary(self, *values):
        names = list(self.running)
        given = [self.pending[name] for name in names]
        held = [value for value in given if value is not None]
        tied = lax.optimization_barrier(tuple(values) + tuple(held))
        passed = list(tied[len(values) :])
        for name, value in zip(names, given):
            self.resume(name, None if value is None else passed.pop(0))
        return tied[: len(values)]

    def finish(self):
        while self.running:
            for name in list(self.running):
                self.resume(name, self.pending[name])


def on_device(
    section_edges,
    lengths,
    joint_weight,
    query_bias,
    value_bias,
    output_weight,
    output_bias,
    first_gain,
    first_shift,
    expand_weight,
    expand_bias,
    reduce_weight,
    reduce_bias,
    second_gain,
    second_shift,
):
    core = lax.axis_index("section")
    first_core = core == 0
    edges = section_edges[0]
    micro_count, seq_count, seq_span, model_width = edges.shape
    row_count = seq_count * seq_span
    edges = edges.reshape(micro_count, row_count, model_width)
    kept_edge = pick(edges, core)
    other_edge = swap(pick(edges, 1 - core), "section")
    hidden = jnp.where(first_core, kept_edge, other_edge)
    cotangent = jnp.where(first_core, other_edge, kept_edge)
    seq_lengths = pick(lengths, core)

    def both_layers(own):
        other = swap(own, "section")
        return (jnp.where(first_core, own, other), jnp.where(first_core, other, own))

    vector_list = (
        query_bias,
        value_bias,
        output_bias,
        first_gain,
        first_shift,
        reduce_bias,
        second_gain,
        second_shift,
        expand_bias,
    )
    cuts = []
    for vector in vector_list:
        cuts.append((cuts[-1] if cuts else 0) + vector.shape[1])
    vector_layers = [
        jnp.split(layer, cuts[:-1])
        for layer in both_layers(jnp.concatenate([v[0] for v in vector_list]))
    ]
    joint_rows, joint_sent = gather_rows(joint_weight[0], True)
    output_rows, output_sent = gather_rows(output_weight[0], False)
    expand_rows, expand_sent = gather_rows(expand_weight[0], False, joint_sent, output_sent)
    reduce_rows, _ = gather_rows(reduce_weight[0], False, expand_sent)
    matrix_layers = list(
        zip(
            both_layers(joint_rows),
            both_layers(output_rows),
            both_layers(expand_rows),
            both_layers(reduce_rows),
        )
    )
    stored_list = []
    for layer in range(2):
        output, stored = layer_forward(
            hidden, seq_lengths, matrix_layers[layer], vector_layers[layer]
        )
        stored_list.append(stored)
        hidden = output.astype(LOWER)
    gradient = cotangent.astype(WIDE)
    sums = Sums()
    vector_terms = [None, None]
    for layer in (1, 0):
        gradient, vector_terms[layer] = layer_backward(
            gradient,
            stored_list[layer],
            seq_lengths,
            matrix_layers[layer],
            vector_layers[layer],
            sums,
            layer,
        )
        if layer == 1:
            gradient = gradient.astype(LOWER).astype(WIDE)
    sums.finish()
    own_rows = jnp.where(first_core, gradient, output)
    other_rows = swap(jnp.where(first_core, output, gradient), "section")
    boundary = put(put(jnp.zeros((2,) + own_rows.shape, WIDE), own_rows, core), other_rows, 1 - core)
    boundary = boundary.reshape(1, micro_count, seq_count, seq_span, model_width)
    positions = lax.axis_size("dp") * lax.axis_size("grid")
    factor = 1.0 / math.sqrt(micro_count * row_count * positions)
    matrix_grads = []
    for index in range(4):
        first_half, second_half = sums.results[0, index], sums.results[1, index]
        kept = jnp.where(first_core, first_half, second_half)
        received = swap(jnp.where(first_core, second_half, first_half), "section")
        whole = put(put(jnp.zeros((2,) + kept.shape, WIDE), kept, core), received, 1 - core)
        matrix_grads.append((whole.reshape(-1, kept.shape[-1]) * factor)[None])
    vector_sum = jnp.where(first_core, vector_terms[0], vector_terms[1]) + swap(
        jnp.where(first_core, vector_terms[1], vector_terms[0]), "section"
    )
    for axis in ("dp", "grid"):
        distance = 1
        while distance < lax.axis_size(axis):
            vector_sum = vector_sum + swap(vector_sum, axis, distance)
            distance *= 2
    vector_grads = [part[None] for part in jnp.split(vector_sum * factor, cuts[:-1])]
    return (
        boundary,
        matrix_grads[0],
        vector_grads[0],
        vector_grads[1],
        matrix_grads[1],
        vector_grads[2],
        vector_grads[3],
        vector_grads[4],
        matrix_grads[2],
        vector_grads[8],
        matrix_grads[3],
        vector_grads[5],
        vector_grads[6],
        vector_grads[7],
    )


def solution(mesh):
    placed = (
        P("section", None, ("dp", "grid"), None, None),
        P(None, ("dp", "grid")),
        P("section", "grid", None),
        P("section", None),
        P("section", None),
        P("section", "grid", None),
        P("section", None),
        P("section", None),
        P("section", None),
        P("section", "grid", None),
        P("section", None),
        P("section", "grid", None),
        P("section", None),
        P("section", None),
        P("section", None),
    )
    return jax.shard_map(
        on_device,
        mesh=mesh,
        in_specs=placed,
        out_specs=(
            P("section", None, ("dp", "grid"), None, None),
            P("section", "grid", None),
            P("section", None),
            P("section", None),
            P("section", "grid", None),
            P("section", None),
            P("section", None),
            P("section", None),
            P("section", "grid", None),
            P("section", None),
            P("section", "grid", None),
            P("section", None),
            P("section", None),
            P("section", None),
        ),
        check_vma=False,
    )
```
